32 devices in a mesh: expert: 8 (over z, y), group: 4 (over x, core).
Axes of the slice: x: 2, y: 2, z: 4, core: 2. Of those that a mesh axis runs over, the one named last changes fastest.
Arguments:
- tokens: bfloat16 [2, 4096, 2048], P(None, ('expert', 'group')), may hold values from -6 to 6
- expert_ids: int32 [2, 4096, 8], P(None, ('expert', 'group')), may hold values from 0 to 31, all different within a row; in each aligned block of 128 rows (0 to 127, 128 to 255, ..., all dimensions but the last counted through in order) at most 40 rows name the same one
- gate_probs: float32 [2, 4096, 8], P(None, ('expert', 'group')), may hold values from 0.05 to 1
- capacity: int32 [32], P(('expert', 'group')), may hold values from 448 to 896, as said below
- flows: int32 [32, 3], P(('expert', 'group')), may hold values from 0 to 64, as said below
- w_gate: bfloat16 [32, 2048, 768], P(('expert', 'group')), may hold values from -0.125 to 0.125
- w_up: bfloat16 [32, 2048, 768], P(('expert', 'group')), may hold values from -0.125 to 0.125
- w_down: bfloat16 [32, 768, 2048], P(('expert', 'group')), may hold values from -0.21875 to 0.21875
Outputs:
- mixed: bfloat16 [2, 4096, 2048], P(None, ('expert', 'group'))
The draws below stay inside these ranges and needn't reach their ends.
Inputs may be any that keep to these rules, and one draw needn't show every extreme that they name: `expert_ids`: among one device's 128 tokens of a micro-batch no expert is chosen more than 40 times, a bound that some block reaches; a token never chooses an expert twice. Some expert has capacity exactly 896. `flows`: some expert has all its grants exactly 64, the same expert that has capacity 896.
All inputs are finite; a program needn't handle non-finite values.
Results may differ from the reference program's by a relative error of at most 0.0085.
Values may be sent and summed in bfloat16 or wider, within the bound.
A program may use at most 128 MiB of HBM per device.

```python
import math
import jax
import jax.numpy as jnp
import numpy as np
from jax import lax

D = 2048
FF = 768
TOPK = 8
TOK_DEV = 128
MICRO = 2
PARTNERS = 3
EXPERTS = 32
TOKENS = 4096
SLOTS = 40
CAP_MAX = 896
FLOW_MAX = 64


def chosen_expert(key):
    return jax.random.randint(jax.random.fold_in(key, 11), (), 0, EXPERTS)


def draw_capacity(key, part):
    drawn = jax.random.randint(jax.random.fold_in(key, 3), (EXPERTS,), CAP_MAX // 2, CAP_MAX + 1)
    return jnp.where(jnp.arange(EXPERTS) == chosen_expert(key), CAP_MAX, drawn).astype(jnp.int32)


def draw_flows(key, part):
    drawn = jax.random.randint(jax.random.fold_in(key, 5), (EXPERTS, PARTNERS), 0, FLOW_MAX + 1)
    picked = (jnp.arange(EXPERTS) == chosen_expert(key))[:, None]
    return jnp.where(picked, FLOW_MAX, drawn).astype(jnp.int32)


def level_of(stream_key, shape, cuts, low, top_value):
    level = 1.0
    for axis_at, parts in cuts:
        draws = jax.random.uniform(jax.random.fold_in(jax.random.fold_in(stream_key, 6), axis_at), (parts,), jnp.float32, low / len(cuts), top_value / len(cuts))
        level = level * jnp.repeat(jnp.exp(draws), shape[axis_at] // parts).reshape((-1,) + (1,) * (len(shape) - 1 - axis_at))
    return level


def deal_out(rng, own, number, rows, number_of, top, reach, slope):
    ranking = jax.random.permutation(rng, number_of)
    crowded, ordinary = shares(number_of, rows * top, reach, slope, True), shares(number_of, rows * top, reach, slope, False)
    places = jnp.arange(number_of)

    def named(tallies, rotation):
        used = int((tallies > 0).sum())
        fixed = max(1, used // 4)
        moved = fixed + (places - fixed + rotation * (used - fixed)) % max(1, number_of - fixed)
        return jnp.zeros((number_of,), jnp.int32).at[ranking[jnp.where(places < fixed, places, moved)]].set(jnp.asarray(tallies, jnp.int32))

    tallies = jnp.where(number % 4 == 0, named(crowded, number // 4), named(ordinary, number - number // 4 - 1))
    mixed = jax.random.permutation(jax.random.fold_in(own, 3), number_of)
    giver, receiver = mixed[0:number_of // 2 * 2:2], mixed[1:number_of // 2 * 2:2]
    slack = jnp.minimum(tallies[giver] - 1, reach - tallies[receiver]) // 2
    slack = jnp.where((giver == ranking[0]) | (receiver == ranking[0]) | (tallies[receiver] == 0), 0, jnp.maximum(slack, 0))
    moved = jax.random.randint(jax.random.fold_in(own, 4), (number_of // 2,), 0, 1 << 20) % (slack + 1)
    tallies = tallies.at[giver].add(-moved).at[receiver].add(moved)
    labels = jnp.searchsorted(jnp.cumsum(tallies), jnp.arange(rows * top), side="right").astype(jnp.int32)
    grid = labels.reshape(top, rows).T
    grid = grid[jax.random.permutation(jax.random.fold_in(own, 1), rows)]
    rotation = jax.random.randint(jax.random.fold_in(own, 2), (rows, 1), 0, top)
    return jnp.take_along_axis(grid, (jnp.arange(top)[None, :] + rotation) % top, axis=1)


def shares(number_of, total, limit, skew, full):
    portions = [(1 << 20) // math.isqrt(rank ** skew) + 1 for rank in range(1, number_of + 1)]
    largest = limit if full else min(limit, max(-(-total // number_of), total * portions[0] // sum(portions)))
    least = 1 if total - largest >= number_of - 1 else 0
    holding, surplus = [largest] + [least] * (number_of - 1), total - largest - least * (number_of - 1)
    while surplus > 0:
        candidates = [i for i in range(1, number_of) if holding[i] < largest] or [i for i in range(1, number_of) if holding[i] < limit]
        mass, remaining = sum([portions[i] for i in candidates]), surplus
        for i in candidates:
            addition = min(limit - holding[i], max(1, remaining * portions[i] // mass), surplus)
            holding[i] = holding[i] + addition
            surplus = surplus - addition
    return np.array(holding)


def scatter_about(key, extent, width, bound, split=(), held_as=jnp.bfloat16):
    entries = jax.random.normal(key, extent, jnp.float32) * width
    if len(split) > 0:
        entries = level_of(key, extent, split, -0.22, 0.18) * entries
    return jnp.clip(entries, min=-bound, max=bound).astype(held_as)


def setup_inputs(seed: int = 0) -> dict:
    seeds = jax.random.split(jax.random.key(seed), 9)
    tokens = scatter_about(seeds[0], (MICRO, TOKENS, D), 1.0, 6.0, ((1, 32),))
    expert_ids_keys = jax.random.split(jax.random.fold_in(seeds[1], 1), MICRO * TOKENS // TOK_DEV)
    expert_ids_turns = jax.random.permutation(jax.random.fold_in(seeds[1], 3), MICRO * TOKENS // TOK_DEV)
    expert_ids = jax.vmap(lambda own, number: deal_out(jax.random.fold_in(seeds[1], 2), own, number, TOK_DEV, EXPERTS, TOPK, SLOTS, 2))(expert_ids_keys, expert_ids_turns).reshape((MICRO, TOKENS, TOPK))
    gate_probs = jnp.clip(jnp.exp(math.log(1.0) - 2.9957323 * jax.random.uniform(seeds[2], (MICRO, TOKENS, TOPK), jnp.float32) ** level_of(seeds[2], (MICRO, TOKENS, TOPK), ((1, 32),), -0.2, 0.2)), 0.05, 1.0)
    capacity = draw_capacity(jax.random.fold_in(seeds[8], 71), 0)
    flows = draw_flows(jax.random.fold_in(seeds[8], 71), 0)
    w_gate = scatter_about(seeds[5], (EXPERTS, D, FF), D ** -0.5, 0.125, ((0, 32),))
    w_up = scatter_about(seeds[6], (EXPERTS, D, FF), D ** -0.5, 0.125, ((0, 32),))
    w_down = scatter_about(seeds[7], (EXPERTS, FF, D), FF ** -0.5, 0.21875, ((0, 32),))
    return {"tokens": tokens, "expert_ids": expert_ids, "gate_probs": gate_probs, "capacity": capacity, "flows": flows, "w_gate": w_gate, "w_up": w_up, "w_down": w_down}


def swiglu_rows(rows_in, gate_mat, up_mat, down_mat):
    gate_val = jnp.dot(rows_in, gate_mat, preferred_element_type=jnp.float32)
    up_val = jnp.dot(rows_in, up_mat, preferred_element_type=jnp.float32)
    hidden = (jax.nn.silu(gate_val) * up_val).astype(jnp.bfloat16)
    return jnp.dot(hidden, down_mat, preferred_element_type=jnp.float32).astype(jnp.bfloat16)


def reference(tokens, expert_ids, gate_probs, capacity, flows, w_gate, w_up, w_down):
    keep_rows = CAP_MAX + PARTNERS * FLOW_MAX
    keep_limit = capacity + jnp.sum(flows, 1)
    expert_iota = jnp.arange(EXPERTS, dtype=jnp.int32)
    results = []
    for micro_index in range(MICRO):
        local_rows = tokens[micro_index]
        pair_expert = expert_ids[micro_index].reshape(-1)
        pair_total = pair_expert.shape[0]
        onehot = (pair_expert[:, None] == expert_iota[None, :]).astype(jnp.int32)
        pair_rank = jnp.sum((jnp.cumsum(onehot, 0) - onehot) * onehot, 1).astype(jnp.int32)
        keep_pair = pair_rank < keep_limit[pair_expert]
        target_row = jnp.where(keep_pair, pair_expert, EXPERTS).astype(jnp.int32)
        probs = gate_probs[micro_index]
        gate_norm = (probs / jnp.sum(probs, 1, keepdims=True)).reshape(-1)
        pair_table = jnp.zeros((EXPERTS, keep_rows), jnp.int32).at[target_row, pair_rank].set(
            jnp.arange(pair_total, dtype=jnp.int32), mode="drop")
        weight_table = jnp.zeros((EXPERTS, keep_rows), gate_norm.dtype).at[target_row, pair_rank].set(
            gate_norm, mode="drop")

        def one_expert(accum_out, packed):
            pair_list, weight_list, gate_mat, up_mat, down_mat = packed
            token_list = pair_list // TOPK
            expert_out = swiglu_rows(local_rows[token_list], gate_mat, up_mat, down_mat)
            added = weight_list[:, None] * expert_out.astype(jnp.float32)
            return accum_out.at[token_list].add(added), None

        accum_out, unused = lax.scan(one_expert, jnp.zeros(local_rows.shape, jnp.float32),
                                     (pair_table, weight_table, w_gate, w_up, w_down))
        results.append(accum_out.astype(jnp.bfloat16))
    return jnp.stack(results)
```

```python
import jax
import jax.numpy as jnp
from jax import lax
from jax.sharding import PartitionSpec as P

AXES = ("expert", "group")


def swiglu_rows(rows_in, gate_mat, up_mat, down_mat):
    gate_val = jnp.dot(rows_in, gate_mat, preferred_element_type=jnp.float32)
    up_val = jnp.dot(rows_in, up_mat, preferred_element_type=jnp.float32)
    hidden = (jax.nn.silu(gate_val) * up_val).astype(jnp.bfloat16)
    return jnp.dot(hidden, down_mat, preferred_element_type=jnp.float32).astype(jnp.bfloat16)


def sparse_body(tokens, expert_ids, gate_probs, capacity, flows, w_gate, w_up, w_down):
    device_count = lax.axis_size(AXES)
    micro_count, tok_local, model_dim = tokens.shape
    top_count = expert_ids.shape[2]
    slot_count = tok_local * top_count * 5 // (4 * device_count)
    slot_total = device_count * slot_count
    keep_limit = capacity[0] + jnp.sum(flows[0])
    expert_iota = jnp.arange(device_count, dtype=jnp.int32)
    slot_all = jnp.arange(slot_total, dtype=jnp.int32)
    slot_iota = jnp.arange(slot_count, dtype=jnp.int32)
    zero_row = jnp.zeros((), jnp.bfloat16)
    results = []
    for micro_index in range(micro_count):
        local_rows = tokens[micro_index]
        pair_expert = expert_ids[micro_index].reshape(-1)
        onehot = (pair_expert[:, None] == expert_iota[None, :]).astype(jnp.int32)
        slot_rank = jnp.sum((jnp.cumsum(onehot, 0) - onehot) * onehot, 1)
        counts = jnp.sum(onehot, 0)
        flat_slot = pair_expert * slot_count + slot_rank
        matches = (flat_slot[:, None] == slot_all[None, :]).reshape(
            tok_local, top_count, slot_total
        )
        select = jnp.any(matches, 1).astype(jnp.bfloat16)
        outgoing = lax.dot_general(
            select, local_rows, (((0,), (0,)), ((), ())), preferred_element_type=jnp.float32
        ).astype(jnp.bfloat16)
        outgoing = outgoing.reshape(device_count, slot_count, model_dim)
        incoming, arrived_counts = (
            lax.all_to_all(outgoing, AXES, split_axis=0, concat_axis=0, tiled=True),
            lax.all_to_all(counts, AXES, split_axis=0, concat_axis=0, tiled=True),
        )
        offset = jnp.cumsum(arrived_counts) - arrived_counts
        back_pos = offset[:, None] + slot_iota[None, :]
        back_live = (slot_iota[None, :] < arrived_counts[:, None]) & (back_pos < keep_limit)
        expert_out = swiglu_rows(
            incoming.reshape(slot_total, model_dim), w_gate[0], w_up[0], w_down[0]
        )
        returned = jnp.where(back_live.reshape(-1)[:, None], expert_out, zero_row)
        returned = returned.reshape(device_count, slot_count, model_dim)
        answered = lax.all_to_all(returned, AXES, split_axis=0, concat_axis=0, tiled=True)
        answered = answered.reshape(slot_total, model_dim)
        probs = gate_probs[micro_index]
        gate_norm = probs / jnp.sum(probs, 1, keepdims=True)
        weights = jnp.sum(matches.astype(jnp.float32) * gate_norm[:, :, None], 1)
        weight_high = weights.astype(jnp.bfloat16)
        weight_low = (weights - weight_high.astype(jnp.float32)).astype(jnp.bfloat16)
        mixed = jnp.dot(weight_high, answered, preferred_element_type=jnp.float32)
        mixed = mixed + jnp.dot(weight_low, answered, preferred_element_type=jnp.float32)
        results.append(mixed.astype(jnp.bfloat16))
    return jnp.stack(results)


def route(expert_ids, gate_probs, keep_limit, device_count):
    gate_norm = gate_probs / jnp.sum(gate_probs, 2, keepdims=True)
    expert_iota = jnp.arange(device_count, dtype=jnp.int32)
    named = expert_ids[:, :, :, None] == expert_iota
    chosen = jnp.any(named, 2).astype(jnp.float32)
    spread = jnp.sum(jnp.where(named, gate_norm[:, :, :, None], 0.0), 2)
    packed = jnp.transpose(jnp.stack([chosen, spread]), (3, 0, 1, 2))
    arrived = lax.all_to_all(packed, AXES, split_axis=0, concat_axis=0, tiled=True)
    chosen, weight = arrived[:, 0], arrived[:, 1]
    tok_local = chosen.shape[2]
    tok_iota = jnp.arange(tok_local, dtype=jnp.int32)
    before = (tok_iota[:, None] < tok_iota[None, :]).astype(jnp.bfloat16)
    rank = jnp.einsum(
        "dmt,tu->dmu", chosen.astype(jnp.bfloat16), before, preferred_element_type=jnp.float32
    )
    counts = jnp.sum(chosen, 2)
    earlier = expert_iota[:, None] < expert_iota[None, :]
    offset = jnp.sum(jnp.where(earlier[:, :, None], counts[:, None, :], 0.0), 0)
    kept = (chosen > 0) & (offset[:, :, None] + rank < keep_limit.astype(jnp.float32))
    slot = jnp.where(kept, rank, -1.0).astype(jnp.int32)
    return slot, weight


def dense_body(tokens, expert_ids, gate_probs, capacity, flows, w_gate, w_up, w_down):
    device_count = lax.axis_size(AXES)
    micro_count, tok_local, model_dim = tokens.shape
    top_count = expert_ids.shape[2]
    slot_count = tok_local * top_count * 5 // (4 * device_count)
    slot_total = device_count * slot_count
    keep_limit = capacity[0] + jnp.sum(flows[0])
    slot_iota = jnp.arange(slot_count, dtype=jnp.int32)
    slot, weight = route(expert_ids, gate_probs, keep_limit, device_count)
    results = []
    for micro_index in range(micro_count):
        gathered = lax.all_gather(tokens[micro_index], AXES, axis=0, tiled=False)
        match = slot[:, micro_index, None, :] == slot_iota[None, :, None]
        select = match.astype(jnp.bfloat16)
        rows = jnp.einsum(
            "dst,dtk->dsk", select, gathered, preferred_element_type=jnp.float32
        ).astype(jnp.bfloat16)
        expert_out = swiglu_rows(
            rows.reshape(slot_total, model_dim), w_gate[0], w_up[0], w_down[0]
        )
        slot_weight = jnp.sum(jnp.where(match, weight[:, micro_index, None, :], 0.0), 2)
        scaled = expert_out.astype(jnp.float32) * slot_weight.reshape(-1)[:, None]
        scaled = scaled.astype(jnp.bfloat16).reshape(device_count, slot_count, model_dim)
        partial = jnp.einsum(
            "dst,dsk->dtk", select, scaled, preferred_element_type=jnp.float32
        ).astype(jnp.bfloat16)
        results.append(lax.psum_scatter(partial, AXES, scatter_dimension=0, tiled=False))
    return jnp.stack(results)


def solution(mesh):
    placed = (
        P(None, AXES, None),
        P(None, AXES, None),
        P(None, AXES, None),
        P(AXES),
        P(AXES, None),
        P(AXES, None, None),
        P(AXES, None, None),
        P(AXES, None, None),
    )

    def chosen_body(*args):
        dense = 4 * args[1].shape[2] >= lax.axis_size(AXES)
        return (dense_body if dense else sparse_body)(*args)

    return jax.shard_map(
        chosen_body,
        mesh=mesh,
        in_specs=placed,
        out_specs=P(None, AXES, None),
        check_vma=False,
    )
```

```python
import jax
import jax.numpy as jnp
from jax import lax
from jax.sharding import PartitionSpec as P

AXES = ("expert", "group")


def swiglu_rows(rows_in, gate_mat, up_mat, down_mat):
    gate_val = jnp.dot(rows_in, gate_mat, preferred_element_type=jnp.float32)
    up_val = jnp.dot(rows_in, up_mat, preferred_element_type=jnp.float32)
    hidden = (jax.nn.silu(gate_val) * up_val).astype(jnp.bfloat16)
    return jnp.dot(hidden, down_mat, preferred_element_type=jnp.float32).astype(jnp.bfloat16)


def route(expert_ids, gate_probs, capacity, flows, planes, slot_count):
    device_count = lax.axis_size(AXES)
    plane_size = device_count // planes
    micro_count, tok_local, top_count = expert_ids.shape
    me = lax.axis_index(AXES)
    my_z, my_spot = me // plane_size, me % plane_size
    expert_iota = jnp.arange(device_count, dtype=jnp.int32)
    gate_norm = gate_probs / jnp.sum(gate_probs, 2, keepdims=True)
    named = expert_ids[:, None] == expert_iota[None, :, None, None]
    spread = jnp.sum(jnp.where(named, gate_norm[:, None], 0.0), 3)
    limit = (capacity[0] + jnp.sum(flows[0])).astype(jnp.float32)
    limit_row = jnp.full((micro_count, 1, tok_local), limit)
    everyone = lax.all_gather(jnp.concatenate([spread, limit_row], 1), AXES, axis=0)
    limits = everyone[:, 0, device_count, 0]
    everyone = everyone[:, :, :device_count]
    here = lax.dynamic_slice_in_dim(everyone, my_z * plane_size, plane_size, 2)
    limits = lax.dynamic_slice_in_dim(limits, my_z * plane_size, plane_size, 0)
    counts = jnp.sum((here > 0).astype(jnp.float32), 3)
    earlier = (expert_iota[:, None] < expert_iota[None, :]).astype(jnp.float32)
    offset = jnp.sum(earlier[:, :, None, None] * counts[:, None], 0)

    def column(value):
        grid = value.reshape((planes, plane_size) + value.shape[1:])
        mine = lax.dynamic_index_in_dim(grid, my_spot, 1, keepdims=False)
        return jnp.roll(mine, -my_z, 0)

    weight, offset = column(here), column(offset)
    chosen = weight > 0
    tok_iota = jnp.arange(tok_local, dtype=jnp.int32)
    before = (tok_iota[:, None] < tok_iota[None, :]).astype(jnp.bfloat16)
    rank = jnp.einsum(
        "jmet,tu->jmeu", chosen.astype(jnp.bfloat16), before, preferred_element_type=jnp.float32
    )
    kept = chosen & (rank + offset[:, :, :, None] < limits[None, None, :, None])
    block = (jnp.arange(planes, dtype=jnp.int32) * slot_count)[:, None, None, None]
    code = jnp.where(chosen, block + rank.astype(jnp.int32), -1)
    weight = jnp.where(kept, weight, 0.0)

    def flat(value):
        value = jnp.transpose(value, (1, 2, 0, 3))
        return value.reshape(micro_count, plane_size, planes * tok_local)

    return flat(code), flat(weight)


def body(tokens, expert_ids, gate_probs, capacity, flows, w_gate, w_up, w_down):
    device_count, group_size = lax.axis_size(AXES), lax.axis_size("group")
    width = max(1, group_size // 2)
    planes = max(1, lax.axis_size("expert") // width)
    plane_size = device_count // planes
    micro_count, tok_local, model_dim = tokens.shape
    top_count = expert_ids.shape[2]
    slot_count = tok_local * top_count * 5 // (4 * device_count)
    sent = planes * slot_count
    plane_groups = [
        [z * plane_size + spot for spot in range(plane_size)] for z in range(planes)
    ]

    def shift(value, step):
        pairs = [
            ((z + step) % planes * plane_size + spot, z * plane_size + spot)
            for z in range(planes)
            for spot in range(plane_size)
        ]
        return lax.ppermute(value, AXES, pairs)

    def swap(value):
        return lax.all_to_all(
            value, AXES, split_axis=0, concat_axis=0, tiled=True, axis_index_groups=plane_groups
        )

    code, weight = route(expert_ids, gate_probs, capacity, flows, planes, slot_count)
    slot_iota = jnp.arange(sent, dtype=jnp.int32)

    columns = []
    for micro_index in range(micro_count):
        own = tokens[micro_index]
        if columns:
            own, columns[-1] = lax.optimization_barrier((own, columns[-1]))
        columns.append([own] + [shift(own, step) for step in range(1, planes)])

    arrived, matches = [], []
    for micro_index in range(micro_count):
        match = code[micro_index][:, None, :] == slot_iota[None, :, None]
        matches.append(match)
        rows = jnp.dot(
            match.astype(jnp.bfloat16).reshape(plane_size * sent, planes * tok_local),
            jnp.concatenate(columns[micro_index], 0),
            preferred_element_type=jnp.float32,
        ).astype(jnp.bfloat16)
        arrived.append(swap(rows.reshape(plane_size, sent, model_dim)))

    answers = []
    for micro_index in range(micro_count):
        expert_out = swiglu_rows(
            arrived[micro_index].reshape(plane_size * sent, model_dim),
            w_gate[0], w_up[0], w_down[0],
        )
        answers.append(swap(expert_out.reshape(plane_size, sent, model_dim)))

    results = []
    for micro_index in range(micro_count):
        back = answers[micro_index].reshape(plane_size * sent, model_dim)
        spread = jnp.where(matches[micro_index], weight[micro_index][:, None, :], 0.0)
        spread = spread.reshape(plane_size * sent, planes * tok_local)
        high = spread.astype(jnp.bfloat16)
        low = (spread - high.astype(jnp.float32)).astype(jnp.bfloat16)
        contract = (((0,), (0,)), ((), ()))
        partial = lax.dot_general(high, back, contract, preferred_element_type=jnp.float32)
        partial = partial + lax.dot_general(low, back, contract, preferred_element_type=jnp.float32)
        partial = partial.reshape(planes, tok_local, model_dim)
        total = partial[0]
        rounded = partial.astype(jnp.bfloat16)
        for step in range(1, planes):
            total = total + shift(rounded[step], -step).astype(jnp.float32)
        results.append(total.astype(jnp.bfloat16))
    return jnp.stack(results)


def solution(mesh):
    placed = (
        P(None, AXES, None),
        P(None, AXES, None),
        P(None, AXES, None),
        P(AXES),
        P(AXES, None),
        P(AXES, None, None),
        P(AXES, None, None),
        P(AXES, None, None),
    )
    return jax.shard_map(
        body,
        mesh=mesh,
        in_specs=placed,
        out_specs=P(None, AXES, None),
        check_vma=False,
    )
```

```python
import jax
import jax.numpy as jnp
from jax import lax
from jax.sharding import PartitionSpec as P

AXES = ("expert", "group")


def body(tokens, expert_ids, gate_probs, capacity, flows, w_gate, w_up, w_down):
    device_count, group_size = lax.axis_size(AXES), lax.axis_size("group")
    width = max(1, group_size // 2)
    planes = max(1, lax.axis_size("expert") // width)
    plane_size = device_count // planes
    micro_count, tok_local, model_dim = tokens.shape
    top_count = expert_ids.shape[2]
    slot_count = tok_local * top_count * 5 // (4 * device_count)
    sent = planes * slot_count
    column = planes * tok_local
    me = lax.axis_index(AXES)
    my_z, my_spot = me // plane_size, me % plane_size
    pairwise = plane_size <= 16 and plane_size & (plane_size - 1) == 0
    plane_iota = jnp.arange(planes, dtype=jnp.int32)
    spot_iota = jnp.arange(plane_size, dtype=jnp.int32)
    mate = my_spot ^ spot_iota if pairwise else spot_iota
    device_iota = jnp.arange(device_count, dtype=jnp.int32)

    def shift(value, step):
        pairs = [
            ((z + step) % planes * plane_size + spot, z * plane_size + spot)
            for z in range(planes)
            for spot in range(plane_size)
        ]
        return lax.ppermute(value, AXES, pairs)

    def swap(value):
        value = value.reshape(plane_size, sent, value.shape[-1])
        if not pairwise:
            groups = [
                [z * plane_size + spot for spot in range(plane_size)] for z in range(planes)
            ]
            value = lax.all_to_all(
                value, AXES, split_axis=0, concat_axis=0, tiled=True, axis_index_groups=groups
            )
            return [value.reshape(plane_size * sent, value.shape[-1])]
        pieces = [value[0]]
        for k in range(1, plane_size):
            pairs = [
                (z * plane_size + spot, z * plane_size + (spot ^ k))
                for z in range(planes)
                for spot in range(plane_size)
            ]
            pieces.append(lax.ppermute(value[k], AXES, pairs))
        return pieces

    def split(value, parts):
        return jnp.split(value, parts, axis=-1)

    cuts_out = [2 if m == 0 else 1 for m in range(micro_count)]
    cuts_back = [2 if m == micro_count - 1 else 1 for m in range(micro_count)]
    columns, last = [], None
    for micro_index in range(micro_count):
        parts = []
        for own in split(tokens[micro_index], cuts_out[micro_index]):
            if last is not None:
                own, last = lax.optimization_barrier((own, last))
                holder[-1] = last
            holder = [own] + [shift(own, step) for step in range(1, planes)]
            last = holder[-1]
            parts.append(holder)
        columns.append(parts)

    gate_norm = gate_probs / jnp.sum(gate_probs, 2, keepdims=True)
    toward = ((my_z - plane_iota) % planes)[:, None] * plane_size + mate[None, :]
    named = expert_ids[None, :, None] == toward[:, None, :, None, None]
    spread = jnp.sum(jnp.where(named, gate_norm[None, :, None], 0.0), 4)
    weight = jnp.stack([spread[0]] + [shift(spread[step], step) for step in range(1, planes)])
    chosen = weight > 0
    tok_iota = jnp.arange(tok_local, dtype=jnp.int32)
    before = (tok_iota[:, None] < tok_iota[None, :]).astype(jnp.bfloat16)
    rank = jnp.einsum(
        "jmet,tu->jmeu", chosen.astype(jnp.bfloat16), before, preferred_element_type=jnp.float32
    )
    block = (plane_iota * slot_count)[:, None, None, None]
    code = jnp.where(chosen, block + rank.astype(jnp.int32), -1)
    code = jnp.transpose(code, (1, 2, 0, 3)).reshape(micro_count, plane_size, column)
    weight = jnp.transpose(weight, (1, 2, 0, 3)).reshape(micro_count, plane_size, column)

    counts = jnp.sum(
        (expert_ids.reshape(1, micro_count, -1) == device_iota[:, None, None]).astype(jnp.int32), 2
    )
    counts = lax.all_to_all(counts, AXES, split_axis=0, concat_axis=0, tiled=True)
    from_device = ((my_z + plane_iota) % planes)[None, :] * plane_size + mate[:, None]
    ahead = device_iota[None, None, :] < from_device[:, :, None]
    offset = jnp.sum(jnp.where(ahead[..., None], counts, 0), 2)
    keep_limit = capacity[0] + jnp.sum(flows[0])
    slot_iota = jnp.arange(slot_count, dtype=jnp.int32)
    live = offset[:, :, None, :] + slot_iota[None, None, :, None] < keep_limit
    live = live.reshape(plane_size * sent, micro_count)

    sent_iota = jnp.arange(sent, dtype=jnp.int32)
    arrived, matches = [], []
    for micro_index in range(micro_count):
        match = code[micro_index][:, None, :] == sent_iota[None, :, None]
        matches.append(match)
        select = match.astype(jnp.bfloat16).reshape(plane_size * sent, column)
        parts = []
        for holder in columns[micro_index]:
            rows = jnp.dot(
                select, jnp.concatenate(holder, 0), preferred_element_type=jnp.float32
            ).astype(jnp.bfloat16)
            parts.append(swap(rows))
        arrived.append(parts)

    answers = []
    for micro_index in range(micro_count):
        rows = jnp.concatenate([jnp.concatenate(p, 0) for p in arrived[micro_index]], 1)
        gate_val = jnp.dot(rows, w_gate[0], preferred_element_type=jnp.float32)
        up_val = jnp.dot(rows, w_up[0], preferred_element_type=jnp.float32)
        hidden = (jax.nn.silu(gate_val) * up_val).astype(jnp.bfloat16)
        parts = []
        for down in split(w_down[0], cuts_back[micro_index]):
            out = jnp.dot(hidden, down, preferred_element_type=jnp.float32)
            out = jnp.where(live[:, micro_index][:, None], out, 0.0).astype(jnp.bfloat16)
            parts.append(swap(out))
        answers.append(parts)

    results = []
    for micro_index in range(micro_count):
        spread = jnp.where(matches[micro_index], weight[micro_index][:, None, :], 0.0)
        spread = spread.astype(jnp.bfloat16).reshape(plane_size * sent, column)
        parts = []
        for pieces in answers[micro_index]:
            back = jnp.concatenate(pieces, 0)
            contract = (((0,), (0,)), ((), ()))
            others = lax.dot_general(
                spread[:, tok_local:], back, contract, preferred_element_type=jnp.float32
            ).astype(jnp.bfloat16)
            others = others.reshape(planes - 1, tok_local, back.shape[1])
            total = lax.dot_general(
                spread[:, :tok_local], back, contract, preferred_element_type=jnp.float32
            )
            for step in range(1, planes):
                total = total + shift(others[step - 1], -step).astype(jnp.float32)
            parts.append(total.astype(jnp.bfloat16))
        results.append(jnp.concatenate(parts, 1))
    return jnp.stack(results)


def solution(mesh):
    placed = (
        P(None, AXES, None),
        P(None, AXES, None),
        P(None, AXES, None),
        P(AXES),
        P(AXES, None),
        P(AXES, None, None),
        P(AXES, None, None),
        P(AXES, None, None),
    )
    return jax.shard_map(
        body,
        mesh=mesh,
        in_specs=placed,
        out_specs=P(None, AXES, None),
        check_vma=False,
    )
```

```python
import jax
import jax.numpy as jnp
from jax import lax
from jax.sharding import PartitionSpec as P

AXES = ("expert", "group")


def body(tokens, expert_ids, gate_probs, capacity, flows, w_gate, w_up, w_down):
    device_count, group_size = lax.axis_size(AXES), lax.axis_size("group")
    width = max(1, group_size // 2)
    planes = max(1, lax.axis_size("expert") // width)
    plane_size = device_count // planes
    micro_count, tok_local, model_dim = tokens.shape
    top_count = expert_ids.shape[2]
    slot_count = tok_local * top_count * 5 // (4 * device_count)
    sent = planes * slot_count
    column = planes * tok_local
    me = lax.axis_index(AXES)
    my_z, my_spot = me // plane_size, me % plane_size
    groups = [[z * plane_size + spot for spot in range(plane_size)] for z in range(planes)]
    plane_iota = jnp.arange(planes, dtype=jnp.int32)
    spot_iota = jnp.arange(plane_size, dtype=jnp.int32)
    device_iota = jnp.arange(device_count, dtype=jnp.int32)

    def shift(value, step):
        pairs = [
            ((z + step) % planes * plane_size + spot, z * plane_size + spot)
            for z in range(planes)
            for spot in range(plane_size)
        ]
        return lax.ppermute(value, AXES, pairs)

    def swap(value):
        value = value.reshape(plane_size, sent, value.shape[-1])
        value = lax.all_to_all(
            value, AXES, split_axis=0, concat_axis=0, tiled=True, axis_index_groups=groups
        )
        return value.reshape(plane_size * sent, value.shape[-1])

    def split(value, parts):
        return jnp.split(value, parts, axis=-1)

    cuts_out = [2 if m == 0 else 1 for m in range(micro_count)]
    cuts_back = [2 if m == micro_count - 1 else 1 for m in range(micro_count)]
    columns, last = [], None
    for micro_index in range(micro_count):
        parts = []
        for own in split(tokens[micro_index], cuts_out[micro_index]):
            if last is not None:
                own, last = lax.optimization_barrier((own, last))
                holder[-1] = last
            holder = [own] + [shift(own, step) for step in range(1, planes)]
            last = holder[-1]
            parts.append(holder)
        columns.append(parts)

    gate_norm = gate_probs / jnp.sum(gate_probs, 2, keepdims=True)
    named = expert_ids[None] == device_iota[:, None, None, None]
    spread = jnp.sum(jnp.where(named, gate_norm[None], 0.0), 3)
    counts = jnp.sum(named.astype(jnp.float32), (2, 3))
    toward = jnp.swapaxes(spread.reshape(planes, plane_size, micro_count, tok_local), 1, 2)
    toward = jnp.broadcast_to(
        toward[:, None], (planes, plane_size, micro_count, plane_size, tok_local)
    ).reshape(device_count, micro_count, plane_size, tok_local)
    tally = jnp.broadcast_to(
        counts[:, :, None, None], (device_count, micro_count, 1, tok_local)
    )
    arrived = lax.all_to_all(
        jnp.concatenate([toward, tally], 2), AXES, split_axis=0, concat_axis=0, tiled=True
    )
    weight = arrived[:, :, :plane_size].reshape((planes, plane_size) + toward.shape[1:])
    weight = lax.dynamic_index_in_dim(weight, my_spot, 1, keepdims=False)
    weight = jnp.roll(weight, -my_z, 0)
    chosen = weight > 0
    tok_iota = jnp.arange(tok_local, dtype=jnp.int32)
    before = (tok_iota[:, None] < tok_iota[None, :]).astype(jnp.bfloat16)
    rank = jnp.einsum(
        "jmet,tu->jmeu", chosen.astype(jnp.bfloat16), before, preferred_element_type=jnp.float32
    )
    block = (plane_iota * slot_count)[:, None, None, None]
    code = jnp.where(chosen, block + rank.astype(jnp.int32), -1)
    code = jnp.transpose(code, (1, 2, 0, 3)).reshape(micro_count, plane_size, column)
    weight = jnp.transpose(weight, (1, 2, 0, 3)).reshape(micro_count, plane_size, column)

    counts = arrived[:, :, plane_size, 0]
    from_device = ((my_z + plane_iota) % planes)[None, :] * plane_size + spot_iota[:, None]
    ahead = device_iota[None, None, :] < from_device[:, :, None]
    offset = jnp.sum(jnp.where(ahead[..., None], counts, 0.0), 2).astype(jnp.int32)
    keep_limit = capacity[0] + jnp.sum(flows[0])
    slot_iota = jnp.arange(slot_count, dtype=jnp.int32)
    live = offset[:, :, None, :] + slot_iota[None, None, :, None] < keep_limit
    live = live.reshape(plane_size * sent, micro_count)

    sent_iota = jnp.arange(sent, dtype=jnp.int32)
    slots, matches, leaving = [], [], []
    for micro_index in range(micro_count):
        match = code[micro_index][:, None, :] == sent_iota[None, :, None]
        matches.append(match)
        select = match.astype(jnp.bfloat16).reshape(plane_size * sent, column)
        parts = []
        for holder in columns[micro_index]:
            rows = jnp.dot(
                select, jnp.concatenate(holder, 0), preferred_element_type=jnp.float32
            ).astype(jnp.bfloat16)
            parts.append(swap(rows))
        leaving.append(rows)
        slots.append(parts)

    answers = []
    for micro_index in range(micro_count):
        rows = slots[micro_index]
        if micro_index + 1 < micro_count:
            rows, leaving[micro_index + 1] = lax.optimization_barrier(
                (rows, leaving[micro_index + 1])
            )
        rows = jnp.concatenate(rows, 1)
        gate_val = jnp.dot(rows, w_gate[0], preferred_element_type=jnp.float32)
        up_val = jnp.dot(rows, w_up[0], preferred_element_type=jnp.float32)
        hidden = (jax.nn.silu(gate_val) * up_val).astype(jnp.bfloat16)
        parts = []
        for down in split(w_down[0], cuts_back[micro_index]):
            out = jnp.dot(hidden, down, preferred_element_type=jnp.float32)
            out = jnp.where(live[:, micro_index][:, None], out, 0.0).astype(jnp.bfloat16)
            parts.append(swap(out))
        answers.append(parts)

    results = []
    for micro_index in range(micro_count):
        spread = jnp.where(matches[micro_index], weight[micro_index][:, None, :], 0.0)
        spread = spread.astype(jnp.bfloat16).reshape(plane_size * sent, column)
        parts = []
        for back in answers[micro_index]:
            contract = (((0,), (0,)), ((), ()))
            others = lax.dot_general(
                spread[:, tok_local:], back, contract, preferred_element_type=jnp.float32
            ).astype(jnp.bfloat16)
            others = others.reshape(planes - 1, tok_local, back.shape[1])
            total = lax.dot_general(
                spread[:, :tok_local], back, contract, preferred_element_type=jnp.float32
            )
            for step in range(1, planes):
                total = total + shift(others[step - 1], -step).astype(jnp.float32)
            parts.append(total.astype(jnp.bfloat16))
        results.append(jnp.concatenate(parts, 1))
    return jnp.stack(results)


def solution(mesh):
    placed = (
        P(None, AXES, None),
        P(None, AXES, None),
        P(None, AXES, None),
        P(AXES),
        P(AXES, None),
        P(AXES, None, None),
        P(AXES, None, None),
        P(AXES, None, None),
    )
    return jax.shard_map(
        body,
        mesh=mesh,
        in_specs=placed,
        out_specs=P(None, AXES, None),
        check_vma=False,
    )
```

```python
import jax
import jax.numpy as jnp
from jax import lax
from jax.sharding import PartitionSpec as P

AXES = ("expert", "group")


def body(tokens, expert_ids, gate_probs, capacity, flows, w_gate, w_up, w_down):
    device_count, group_size = lax.axis_size(AXES), lax.axis_size("group")
    width = max(1, group_size // 2)
    planes = max(1, lax.axis_size("expert") // width)
    plane_size = device_count // planes
    micro_count, tok_local, model_dim = tokens.shape
    top_count = expert_ids.shape[2]
    slot_count = tok_local * top_count * 5 // (4 * device_count)
    sent = planes * slot_count
    column = planes * tok_local
    me = lax.axis_index(AXES)
    my_z, my_spot = me // plane_size, me % plane_size
    groups = [[z * plane_size + spot for spot in range(plane_size)] for z in range(planes)]
    plane_iota = jnp.arange(planes, dtype=jnp.int32)
    spot_iota = jnp.arange(plane_size, dtype=jnp.int32)
    device_iota = jnp.arange(device_count, dtype=jnp.int32)

    def shift(value, step):
        pairs = [
            ((z + step) % planes * plane_size + spot, z * plane_size + spot)
            for z in range(planes)
            for spot in range(plane_size)
        ]
        return lax.ppermute(value, AXES, pairs)

    def swap(value):
        value = value.reshape(plane_size, sent, value.shape[-1])
        value = lax.all_to_all(
            value, AXES, split_axis=0, concat_axis=0, tiled=True, axis_index_groups=groups
        )
        return value.reshape(plane_size * sent, value.shape[-1])

    def known(value):
        first = value[(0,) * value.ndim]
        return first == first

    def split(value, parts):
        return jnp.split(value, parts, axis=-1)

    cuts_out = [2 if m == 0 else 1 for m in range(micro_count)]
    cuts_back = [2 if m == micro_count - 1 else 1 for m in range(micro_count)]
    columns, last = [], None
    for micro_index in range(micro_count):
        parts = []
        for own in split(tokens[micro_index], cuts_out[micro_index]):
            if last is not None:
                own, last = lax.optimization_barrier((own, last))
                holder[-1] = last
            holder = [own] + [shift(own, step) for step in range(1, planes)]
            last = holder[-1]
            parts.append(holder)
        columns.append(parts)

    gate_norm = gate_probs / jnp.sum(gate_probs, 2, keepdims=True)
    named = expert_ids[None] == device_iota[:, None, None, None]
    spread = jnp.sum(jnp.where(named, gate_norm[None], 0.0), 3)
    counts = jnp.sum(named.astype(jnp.float32), (2, 3))
    toward = jnp.swapaxes(spread.reshape(planes, plane_size, micro_count, tok_local), 1, 2)
    toward = jnp.broadcast_to(
        toward[:, None], (planes, plane_size, micro_count, plane_size, tok_local)
    ).reshape(device_count, micro_count, plane_size, tok_local)
    tally = jnp.broadcast_to(
        counts[:, :, None, None], (device_count, micro_count, 1, tok_local)
    )
    arrived = lax.all_to_all(
        jnp.concatenate([toward, tally], 2), AXES, split_axis=0, concat_axis=0, tiled=True
    )
    weight = arrived[:, :, :plane_size].reshape((planes, plane_size) + toward.shape[1:])
    weight = lax.dynamic_index_in_dim(weight, my_spot, 1, keepdims=False)
    weight = jnp.roll(weight, -my_z, 0)
    chosen = weight > 0
    tok_iota = jnp.arange(tok_local, dtype=jnp.int32)
    before = (tok_iota[:, None] < tok_iota[None, :]).astype(jnp.bfloat16)
    rank = jnp.einsum(
        "jmet,tu->jmeu", chosen.astype(jnp.bfloat16), before, preferred_element_type=jnp.float32
    )
    block = (plane_iota * slot_count)[:, None, None, None]
    code = jnp.where(chosen, block + rank.astype(jnp.int32), -1)
    code = jnp.transpose(code, (1, 2, 0, 3)).reshape(micro_count, plane_size, column)
    weight = jnp.transpose(weight, (1, 2, 0, 3)).reshape(micro_count, plane_size, column)

    counts = arrived[:, :, plane_size, 0]
    from_device = ((my_z + plane_iota) % planes)[None, :] * plane_size + spot_iota[:, None]
    ahead = device_iota[None, None, :] < from_device[:, :, None]
    offset = jnp.sum(jnp.where(ahead[..., None], counts, 0.0), 2).astype(jnp.int32)
    keep_limit = capacity[0] + jnp.sum(flows[0])
    slot_iota = jnp.arange(slot_count, dtype=jnp.int32)
    live = offset[:, :, None, :] + slot_iota[None, None, :, None] < keep_limit
    live = live.reshape(plane_size * sent, micro_count)

    sent_iota = jnp.arange(sent, dtype=jnp.int32)
    slots, matches, leaving = [], [], []
    for micro_index in range(micro_count):
        match = code[micro_index][:, None, :] == sent_iota[None, :, None]
        matches.append(match)
        select = match.astype(jnp.bfloat16).reshape(plane_size * sent, column)
        parts = []
        for holder in columns[micro_index]:
            rows = jnp.dot(
                select, jnp.concatenate(holder, 0), preferred_element_type=jnp.float32
            ).astype(jnp.bfloat16)
            parts.append(swap(rows))
        leaving.append(rows)
        slots.append(parts)

    def plane_sum(micro_index, back):
        spread = jnp.where(matches[micro_index], weight[micro_index][:, None, :], 0.0)
        spread = spread.astype(jnp.bfloat16).reshape(plane_size * sent, column)
        contract = (((0,), (0,)), ((), ()))
        others = lax.dot_general(
            spread[:, tok_local:], back, contract, preferred_element_type=jnp.float32
        ).astype(jnp.bfloat16)
        own = lax.dot_general(
            spread[:, :tok_local], back, contract, preferred_element_type=jnp.float32
        )
        return others.reshape(planes - 1, tok_local, back.shape[1]), own

    sums = []
    for micro_index in range(micro_count):
        rows = jnp.concatenate(slots[micro_index], 1)
        gate_val = jnp.dot(rows, w_gate[0], preferred_element_type=jnp.float32)
        up_val = jnp.dot(rows, w_up[0], preferred_element_type=jnp.float32)
        hidden = (jax.nn.silu(gate_val) * up_val).astype(jnp.bfloat16)
        parts = []
        for down in split(w_down[0], cuts_back[micro_index]):
            shown = live[:, micro_index]
            if micro_index + 1 < micro_count:
                shown = shown & known(leaving[micro_index + 1])
            if parts and sums:
                shown = shown & known(sums[-1][-1][0]) & known(out)
            out = jnp.dot(hidden, down, preferred_element_type=jnp.float32)
            out = jnp.where(shown[:, None], out, 0.0).astype(jnp.bfloat16)
            parts.append(plane_sum(micro_index, swap(out)))
        sums.append(parts)

    results = []
    for micro_index in range(micro_count):
        parts = []
        for others, total in sums[micro_index]:
            if results:
                others = jnp.where(known(results[-1]), others, 0)
            for step in range(1, planes):
                total = total + shift(others[step - 1], -step).astype(jnp.float32)
            parts.append(total.astype(jnp.bfloat16))
        results.append(jnp.concatenate(parts, 1))
    return jnp.stack(results)


def solution(mesh):
    placed = (
        P(None, AXES, None),
        P(None, AXES, None),
        P(None, AXES, None),
        P(AXES),
        P(AXES, None),
        P(AXES, None, None),
        P(AXES, None, None),
        P(AXES, None, None),
    )
    return jax.shard_map(
        body,
        mesh=mesh,
        in_specs=placed,
        out_specs=P(None, AXES, None),
        check_vma=False,
    )
```
